32 devices in a mesh: req: 8 (over z, y), seq: 4 (over x, core).
Axes of the slice: x: 2, y: 2, z: 4, core: 2. Of those that a mesh axis runs over, the one named last changes fastest.
Arguments:
- queries: bfloat16 [16, 48, 8192], P('req', None, 'seq')
- draft_key_value: bfloat16 [16, 48, 2048], P('req', None, 'seq'), may hold values from -6 to 6
- kv_cache: bfloat16 [16, 8192, 2048], P('req', 'seq')
- cache_lengths: int32 [16], P('req'), may hold values from 2 to 8192, as said below
- ancestors: int32 [16, 48, 48], P('req'), may hold values from 0 to 1, as said below
- dealing: int32 [16], replicated, may hold values from 0 to 15, as said below
- accepted_path: int32 [16, 8], P('req'), may hold values from 0 to 47
Outputs:
- verified_context: bfloat16 [768, 8192], P(('req', 'seq'))
- kept_entries: bfloat16 [16, 8, 2048], P('req', None, 'seq')
The draws below stay inside these ranges and needn't reach their ends.
Inputs may be any that keep to these rules, and one draw needn't show every extreme that they name: `dealing`: a permutation of the request ids. `cache_lengths`: at least 2 live positions; some slot's cache is full (8192). Each row is the 0/1 indicator of a draft token's ancestors in its tree, the token itself included; token 0 is the root, a token's parent has a lower index.
All inputs are finite; a program needn't handle non-finite values.
Results may differ from the reference program's by a relative error of at most 0.0046.
Values may be sent and summed in bfloat16 or wider, within the bound.
A program may use at most 128 MiB of HBM per device.

```python
import jax
import jax.numpy as jnp
from jax import lax

D = 8192
QUERY_HEADS = 64
KEY_HEADS = 8
HEAD_WIDTH = 128
TREE_TOKENS = 48
DEPTH = 8
BLK = 1024
REQUEST_COUNT = 16
CONTEXT_LENGTH = 8192


def dealing_order(key):
    return jax.random.permutation(jax.random.fold_in(key, 11), REQUEST_COUNT).astype(jnp.int32)


def front_rows(key):
    starting_rows = jax.random.normal(jax.random.fold_in(key, 12), (REQUEST_COUNT, KEY_HEADS, 2, HEAD_WIDTH), jnp.float32)
    additional_rows = jax.random.normal(jax.random.fold_in(key, 13), (REQUEST_COUNT, KEY_HEADS, 2, HEAD_WIDTH), jnp.float32)
    mixing = jnp.array([0.99, 0.0], jnp.float32)[:, None]
    fresh = jnp.array([0.1, 1.0], jnp.float32)[:, None]
    next_row_index = starting_rows * mixing + additional_rows * fresh
    return jnp.stack([starting_rows, next_row_index], axis=1).reshape(REQUEST_COUNT, 2, KEY_HEADS * 2 * HEAD_WIDTH)


def draw_kv_cache(key, part):
    complete_cache = jax.random.normal(jax.random.fold_in(key, 14), (REQUEST_COUNT, CONTEXT_LENGTH, KEY_HEADS * 2 * HEAD_WIDTH), jnp.float32)
    complete_cache = complete_cache.at[:, 0:2, :].set(front_rows(key))
    return complete_cache.astype(jnp.bfloat16)


def draw_queries(key, part):
    base_query = jax.random.normal(jax.random.fold_in(key, 15), (REQUEST_COUNT, TREE_TOKENS, QUERY_HEADS, HEAD_WIDTH), jnp.float32)
    return base_query.reshape(REQUEST_COUNT, TREE_TOKENS, QUERY_HEADS * HEAD_WIDTH).astype(jnp.bfloat16)


def draw_dealing(key, part):
    return dealing_order(key)


def draw_cache_lengths(key, part):
    lengths_drawn = jax.random.randint(jax.random.fold_in(key, 16), (REQUEST_COUNT,), 2, CONTEXT_LENGTH + 1, jnp.int32)
    picked = jax.random.randint(jax.random.fold_in(key, 17), (), 0, REQUEST_COUNT, jnp.int32)
    return lengths_drawn.at[picked].set(CONTEXT_LENGTH)


def draw_ancestors(key, part):
    raw_bits = jax.random.randint(jax.random.fold_in(key, 18), (REQUEST_COUNT, TREE_TOKENS), 0, 1 << 20, jnp.int32)
    closure = jnp.broadcast_to(jnp.eye(TREE_TOKENS, dtype=jnp.int32)[None], (REQUEST_COUNT, TREE_TOKENS, TREE_TOKENS))
    for node in range(1, TREE_TOKENS):
        parent = raw_bits[:, node] % node
        inherited = closure[jnp.arange(REQUEST_COUNT), parent]
        closure = closure.at[:, node].set(jnp.maximum(inherited, closure[:, node]))
    return closure


def place_ends(values, own_key, low, largest):
    shape = values.shape
    spot = [jax.random.randint(jax.random.fold_in(own_key, axis), (), 0, shape[axis]) for axis in range(len(shape))]
    values = values.at[tuple(spot)].set(low)
    longest = shape.index(max(shape))
    spot[longest] = (spot[longest] + 1) % shape[longest]
    return values.at[tuple(spot)].set(largest)


def level_of(own_key, extent, cuts, least, high):
    loudness, own = 1.0, jax.random.fold_in(own_key, 6)
    for dim, parts in cuts:
        draws = jnp.exp(jax.random.uniform(jax.random.fold_in(own, dim), (parts,), jnp.float32, least / len(cuts), high / len(cuts)))
        loudness = loudness * jnp.repeat(draws, extent[dim] // parts).reshape([-1 if axis == dim else 1 for axis in range(len(extent))])
    return loudness


def bell_draw(key, shape, spread, bound, split=(), held_as=jnp.bfloat16):
    entries = spread * jax.random.normal(key, shape, jnp.float32)
    if split:
        entries = entries * level_of(key, shape, split, -0.22, 0.18)
    return jnp.clip(entries, -bound, bound).astype(held_as)


def setup_inputs(seed: int = 0) -> dict:
    key_list = jax.random.split(jax.random.key(seed), 8)
    queries = draw_queries(jax.random.fold_in(key_list[7], 71), 0)
    draft_key_value = bell_draw(key_list[1], (REQUEST_COUNT, TREE_TOKENS, KEY_HEADS * 2 * HEAD_WIDTH), 1.0, 6.0, ((0, 8), (2, 4)))
    kv_cache = draw_kv_cache(jax.random.fold_in(key_list[7], 71), 0)
    cache_lengths = draw_cache_lengths(jax.random.fold_in(key_list[7], 71), 0)
    ancestors = draw_ancestors(jax.random.fold_in(key_list[7], 71), 0)
    dealing = draw_dealing(jax.random.fold_in(key_list[7], 71), 0)
    accepted_path = place_ends(jax.random.randint(key_list[6], (REQUEST_COUNT, DEPTH), 0, TREE_TOKENS), jax.random.fold_in(key_list[6], 1), 0, TREE_TOKENS - 1).astype(jnp.int32)
    return {"queries": queries, "draft_key_value": draft_key_value, "kv_cache": kv_cache, "cache_lengths": cache_lengths, "ancestors": ancestors, "dealing": dealing, "accepted_path": accepted_path}


def online_merge(earlier, later):
    max_a, sum_a, acc_a = earlier
    max_b, sum_b, acc_b = later
    row_max = jnp.maximum(max_a, max_b)
    scale_a = jnp.exp(max_a - row_max)
    scale_b = jnp.exp(max_b - row_max)
    return (row_max, sum_a * scale_a + sum_b * scale_b, acc_a * scale_a[..., None] + acc_b * scale_b[..., None])


def block_terms(grouped, key_rows, values, allowed):
    scores = jnp.einsum("tkgd,skd->kgts", grouped.astype(jnp.float32), key_rows.astype(jnp.float32)) * (HEAD_WIDTH ** -0.5)
    scores = jnp.where(allowed, scores, jnp.float32(-1e30))
    row_max = jnp.max(scores, axis=-1)
    weights = jnp.where(allowed, jnp.exp(scores - row_max[..., None]), jnp.float32(0.0))
    row_sum = jnp.sum(weights, axis=-1)
    rounded = weights.astype(jnp.bfloat16).astype(jnp.float32)
    row_acc = jnp.einsum("kgts,skd->kgtd", rounded, values.astype(jnp.float32))
    return row_max, row_sum, row_acc


def attend(query_rows, cache_rows, draft_rows, length, pos_offset, tree_mask, use_draft, blk_size):
    tree_len = query_rows.shape[0]
    kv_heads = cache_rows.shape[1] // (2 * HEAD_WIDTH)
    groups = query_rows.shape[1] // (HEAD_WIDTH * kv_heads)
    grouped = query_rows.reshape(tree_len, kv_heads, groups, HEAD_WIDTH)
    draft_part = draft_rows.reshape(tree_len, kv_heads, 2, HEAD_WIDTH)
    draft_allowed = jnp.logical_and(tree_mask > 0, use_draft)[None, None]
    running = block_terms(grouped, draft_part[:, :, 0], draft_part[:, :, 1], draft_allowed)
    blk_count = cache_rows.shape[0] // blk_size

    def body_step(blk_index, state):
        blk_start = blk_index * blk_size

        def absorb(state_in):
            cache_piece = lax.dynamic_slice_in_dim(cache_rows, blk_start, blk_size, 0).reshape(blk_size, kv_heads, 2, HEAD_WIDTH)
            positions = pos_offset + blk_start + jnp.arange(blk_size, dtype=jnp.int32)
            allowed = (positions < length)[None, None, None, :]
            return online_merge(state_in, block_terms(grouped, cache_piece[:, :, 0], cache_piece[:, :, 1], allowed))

        return lax.cond(pos_offset + blk_start < length, absorb, lambda state_in: state_in, state)

    return lax.fori_loop(0, blk_count, body_step, running)


def reference(queries, draft_key_value, kv_cache, cache_lengths, ancestors, dealing, accepted_path):
    expanded = jnp.broadcast_to(accepted_path[:, :, None], accepted_path.shape + (draft_key_value.shape[2],))
    kept_entries = jnp.take_along_axis(draft_key_value, expanded, axis=1)

    def one_request(slot_index):
        request = dealing[slot_index]
        row_max, row_sum, row_acc = attend(queries[request], kv_cache[slot_index], draft_key_value[request], cache_lengths[slot_index], 0, ancestors[slot_index], True, BLK)
        normed = (row_acc / row_sum[..., None]).transpose(2, 0, 1, 3).reshape(TREE_TOKENS, QUERY_HEADS * HEAD_WIDTH)
        return normed.astype(jnp.bfloat16)

    context = lax.map(one_request, jnp.arange(REQUEST_COUNT, dtype=jnp.int32))
    return context.reshape(REQUEST_COUNT * TREE_TOKENS, D), kept_entries
```

```python
import functools
import math

import jax
import jax.numpy as jnp
from jax import lax
from jax.experimental import pallas as pl
from jax.experimental.pallas import tpu as pltpu
from jax.sharding import PartitionSpec as P

HEAD_WIDTH = 128
BLK = 1024


def online_merge(earlier, later):
    max_a, sum_a, acc_a = earlier
    max_b, sum_b, acc_b = later
    row_max = jnp.maximum(max_a, max_b)
    scale_a = jnp.exp(max_a - row_max)
    scale_b = jnp.exp(max_b - row_max)
    return (
        row_max,
        sum_a * scale_a + sum_b * scale_b,
        acc_a * scale_a[..., None] + acc_b * scale_b[..., None],
    )


def block_terms(grouped, key_rows, values, allowed):
    scores = jnp.einsum(
        "tkgd,skd->tkgs", grouped, key_rows, preferred_element_type=jnp.float32
    ) * HEAD_WIDTH ** (-0.5)
    scores = jnp.where(allowed, scores, jnp.float32(-1e30))
    row_max = jnp.max(scores, axis=-1)
    weights = jnp.where(allowed, jnp.exp(scores - row_max[..., None]), jnp.float32(0.0))
    row_sum = jnp.sum(weights, axis=-1)
    row_acc = jnp.einsum(
        "tkgs,skd->tkgd", weights.astype(jnp.bfloat16), values, preferred_element_type=jnp.float32
    )
    return (row_max, row_sum, row_acc)


def attend(query_rows, cache_rows, draft_rows, length, pos_offset, tree_mask, use_draft, blk_size):
    tree_len = query_rows.shape[0]
    kv_heads = cache_rows.shape[1] // (2 * HEAD_WIDTH)
    groups = query_rows.shape[1] // (HEAD_WIDTH * kv_heads)
    grouped = query_rows.reshape(tree_len, kv_heads, groups, HEAD_WIDTH)
    draft_part = draft_rows.reshape(tree_len, kv_heads, 2, HEAD_WIDTH)
    draft_allowed = jnp.logical_and(tree_mask > 0, use_draft)[:, None, None, :]
    running = block_terms(grouped, draft_part[:, :, 0], draft_part[:, :, 1], draft_allowed)
    blk_count = cache_rows.shape[0] // blk_size

    def body_step(blk_index, state):
        blk_start = blk_index * blk_size

        def absorb(state_in):
            cache_piece = lax.dynamic_slice_in_dim(cache_rows, blk_start, blk_size, 0).reshape(
                blk_size, kv_heads, 2, HEAD_WIDTH
            )
            positions = pos_offset + blk_start + jnp.arange(blk_size, dtype=jnp.int32)
            allowed = (positions < length)[None, None, None, :]
            return online_merge(
                state_in, block_terms(grouped, cache_piece[:, :, 0], cache_piece[:, :, 1], allowed)
            )

        return lax.cond(pos_offset + blk_start < length, absorb, lambda state_in: state_in, state)

    return lax.fori_loop(0, blk_count, body_step, running)


def plain_body(queries, draft_key_value, kv_cache, cache_lengths, ancestors, dealing, accepted_path):
    local_reqs = kv_cache.shape[0]
    tree_len = queries.shape[1]
    picker = (
        accepted_path[:, :, None] == jnp.arange(tree_len, dtype=jnp.int32)[None, None, :]
    ).astype(jnp.bfloat16)
    kept_entries = jnp.einsum(
        "rit,rtc->ric", picker, draft_key_value, preferred_element_type=jnp.float32
    ).astype(jnp.bfloat16)
    every_query, every_draft = (
        lax.all_gather(queries, "req", axis=0, tiled=True),
        lax.all_gather(draft_key_value, "req", axis=0, tiled=True),
    )
    chosen = lax.dynamic_slice_in_dim(dealing, lax.axis_index("req") * local_reqs, local_reqs)
    own_query = jnp.stack(
        [
            lax.dynamic_index_in_dim(every_query, chosen[slot], 0, keepdims=False)
            for slot in range(local_reqs)
        ],
        axis=0,
    )
    own_draft = jnp.stack(
        [
            lax.dynamic_index_in_dim(every_draft, chosen[slot], 0, keepdims=False)
            for slot in range(local_reqs)
        ],
        axis=0,
    )
    seq_count = lax.axis_size("seq")
    full_query, full_draft = (
        lax.all_gather(own_query, "seq", axis=2, tiled=True),
        lax.all_gather(own_draft, "seq", axis=2, tiled=True),
    )
    position = lax.axis_index("seq")
    pos_offset = position * kv_cache.shape[1]
    maxima, sums, partials = ([], [], [])
    for slot_index in range(local_reqs):
        row_max, row_sum, row_acc = attend(
            full_query[slot_index],
            kv_cache[slot_index],
            full_draft[slot_index],
            cache_lengths[slot_index],
            pos_offset,
            ancestors[slot_index],
            position == 0,
            BLK,
        )
        maxima.append(row_max.reshape(tree_len, -1))
        sums.append(row_sum.reshape(tree_len, -1))
        partials.append(row_acc.reshape(tree_len, -1))
    all_max = jnp.concatenate(maxima, axis=0)
    all_sum = jnp.concatenate(sums, axis=0)
    all_acc = jnp.concatenate(partials, axis=0)
    head_count = all_max.shape[1]
    recv_acc, recv_max, recv_sum = (
        lax.all_to_all(all_acc[None], "seq", split_axis=1, concat_axis=0, tiled=True),
        lax.all_to_all(all_max[None], "seq", split_axis=1, concat_axis=0, tiled=True),
        lax.all_to_all(all_sum[None], "seq", split_axis=1, concat_axis=0, tiled=True),
    )
    top_max = jnp.max(recv_max, axis=0)
    factors = jnp.exp(recv_max - top_max[None])
    denominator = jnp.sum(factors * recv_sum, axis=0)
    token_count = recv_acc.shape[1]
    numerator = jnp.sum(
        factors[..., None] * recv_acc.reshape(seq_count, token_count, head_count, HEAD_WIDTH),
        axis=0,
    )
    context = (
        (numerator / denominator[..., None])
        .reshape(token_count, head_count * HEAD_WIDTH)
        .astype(jnp.bfloat16)
    )
    return (context, kept_entries)


MESH = pl.DeviceIdType.MESH
TOK = 48
HALF = TOK // 2
ROWS = 8 * HALF
NEG = -1e30
SCALE2 = HEAD_WIDTH ** (-0.5) * math.log2(math.e)
GROUPS = 8
QUARTERS = 4
ROW_CHUNKS = 2


def fused_kernel(
    deal, lens, q_ref, d_ref, kv_ref, anc_ref, out_ref,
    r1q, r1d, s2q, s2d, qf, df, kvb, accs, rbuf, stats, rstat,
    s1, r1, s1d, r1ds, s2, r2, s2ds, r2ds, cs, cr, xs, xr, fs, fr, kvs,
    os0, os1, os2, ors, ss, srs,
):
    g = lax.axis_index("req")
    q = lax.axis_index("seq")
    xx, cc = q // 2, q % 2
    core = xx * 2 + (1 - cc)
    xpart = (1 - xx) * 2 + cc
    xcore = (1 - xx) * 2 + (1 - cc)

    barrier = pltpu.get_barrier_semaphore()
    for o in range(1, GROUPS):
        pl.semaphore_signal(barrier, inc=1, device_id=(lax.rem(g + o, GROUPS), q), device_id_type=MESH)
    for other in (core, xpart, xcore):
        pl.semaphore_signal(barrier, inc=1, device_id=(g, other), device_id_type=MESH)
    pl.semaphore_wait(barrier, GROUPS + 2)

    def relays(i):
        return i % 2 == (i // 2) % 2

    def remote(src, dst, send, recv, dev):
        return pltpu.make_async_remote_copy(
            src_ref=src, dst_ref=dst, send_sem=send, recv_sem=recv, device_id=dev, device_id_type=MESH
        )

    def first_q(o):
        i = lax.rem(g + o, GROUPS)
        return remote(
            q_ref.at[:, :, pl.ds(pl.multiple_of(i * 256, 256), 256)], r1q.at[pl.ds(2 * g, 2)],
            s1.at[o], r1.at[o], (i, q),
        )

    def first_d(o):
        i = lax.rem(g + o, GROUPS)
        return remote(
            d_ref.at[:, :, pl.ds(pl.multiple_of((i // 2) * 128, 128), 128)], r1d.at[pl.ds(2 * g, 2)],
            s1d.at[o], r1ds.at[o], (i, q),
        )

    def kv_copy(slot, k):
        return pltpu.make_async_copy(
            kv_ref.at[slot, :, pl.ds(pl.multiple_of(k * 256, 256), 256)],
            kvb.at[slot * 8 + k], kvs.at[slot * 8 + k],
        )

    for o in range(1, GROUPS):
        first_q(o).start()

        @pl.when(relays(lax.rem(g + o, GROUPS)))
        def _():
            first_d(o).start()

    def start_kv(n, carry):
        kv_copy(n // 8, n % 8).start()
        return carry

    lax.fori_loop(0, 16, start_kv, 0)
    r1q[pl.ds(2 * g, 2)] = q_ref[:, :, pl.ds(pl.multiple_of(g * 256, 256), 256)]
    r1d[pl.ds(2 * g, 2)] = d_ref[:, :, pl.ds(pl.multiple_of((g // 2) * 128, 128), 128)]
    for part in range(2):
        for half in range(2):
            stats[part, half] = jnp.ones_like(stats[part, half])

    for o in range(1, GROUPS):
        first_q(o).wait_recv()

        @pl.when(relays(g))
        def _():
            first_d(o).wait_recv()

    def second_q(o):
        d = lax.rem(g + o, GROUPS)
        return remote(
            s2q.at[d], qf.at[:, pl.ds(q * 16 + g * 2, 2)], s2.at[o], r2.at[o], (d, q)
        )

    def second_d(o):
        d = lax.rem(g + o, GROUPS)
        return remote(s2d.at[d], df.at[:, g // 2], s2ds.at[o], r2ds.at[o], (d, q))

    for o in list(range(1, GROUPS)) + [0]:
        d = lax.rem(g + o, GROUPS)
        for j in range(2):
            r = deal[2 * d + j]
            piece = r1q[r]
            if o == 0:
                qf[j, q * 16 + g * 2] = piece[:, :128]
                qf[j, q * 16 + g * 2 + 1] = piece[:, 128:]
            else:
                s2q[d, j, 0] = piece[:, :128]
                s2q[d, j, 1] = piece[:, 128:]
        if o:
            second_q(o).start()

        @pl.when(relays(g))
        def _():
            for j in range(2):
                r = deal[2 * d + j]
                if o == 0:
                    df[j, g // 2] = r1d[r]
                else:
                    s2d[d, j] = r1d[r]
            if o:
                second_d(o).start()

    def spread(o, owner, send, recv, to):
        src = lax.rem(g + GROUPS - o, GROUPS)
        part = qf.at[:, pl.ds(owner * 16 + src * 2, 2)]
        return remote(part, part, send.at[o], recv.at[o], (g, to))

    for o in range(GROUPS):
        if o:
            second_q(o).wait_recv()
        spread(o, q, xs, xr, xpart).start()
        spread(o, q, cs, cr, core).start()
    for o in range(1, GROUPS):

        @pl.when(relays(lax.rem(g + GROUPS - o, GROUPS)))
        def _():
            second_d(o).wait_recv()

    def acc_send(slot, half, k, sem, to):
        return remote(accs.at[slot, half, k], rbuf.at[q, k], sem.at[k], ors.at[q, k], (g, to))

    def step(slot, k, own):
        kv_copy(slot, k).wait()
        keys = kvb[slot * 8 + k, :, :128]
        values = jnp.concatenate(
            [kvb[slot * 8 + k, :, 128:], jnp.ones((2048, 128), jnp.bfloat16)], axis=1
        )
        where_pos = lax.broadcasted_iota(jnp.int32, (1, 2048), 1) + q * 2048
        bias = jnp.where(where_pos < lens[slot], jnp.float32(0.0), jnp.float32(NEG))
        tree = jnp.where(
            jnp.logical_and(anc_ref[slot] > 0, jnp.full((TOK, TOK), own, jnp.int32) > 0),
            jnp.float32(0.0), jnp.float32(NEG),
        )
        dk = df[slot, (k % 2) * 2]
        dv = jnp.concatenate([df[slot, (k % 2) * 2 + 1], jnp.ones((TOK, 128), jnp.bfloat16)], axis=1)
        lane = lax.broadcasted_iota(jnp.int32, (HALF, 128), 1)
        heads = 8 // ROW_CHUNKS
        rows = heads * TOK
        contract = (((1,), (1,)), ((), ()))
        for part in range(ROW_CHUNKS):
            qs = qf[slot, pl.ds(k * 8 + part * heads, heads)].reshape(rows, 128)
            s = lax.dot_general(qs, keys, contract, preferred_element_type=jnp.float32) + bias
            t = lax.dot_general(qs, dk, contract, preferred_element_type=jnp.float32)
            t = (t.reshape(heads, TOK, TOK) + tree[None]).reshape(rows, TOK)
            m = jnp.maximum(jnp.max(s, axis=1, keepdims=True), jnp.max(t, axis=1, keepdims=True))
            p = jnp.exp2((s - m) * SCALE2).astype(jnp.bfloat16)
            pt = jnp.exp2((t - m) * SCALE2).astype(jnp.bfloat16)
            o = lax.dot_general(p, values, (((1,), (0,)), ((), ())), preferred_element_type=jnp.float32)
            o = o + lax.dot_general(pt, dv, (((1,), (0,)), ((), ())), preferred_element_type=jnp.float32)
            o3 = o.reshape(heads, TOK, 256)
            m3 = jnp.broadcast_to(m, (rows, 128)).reshape(heads, TOK, 128)
            for half in range(2):
                cut = slice(half * HALF, (half + 1) * HALF)
                accs[slot, half, k, pl.ds(part * heads * HALF, heads * HALF)] = (
                    o3[:, cut, :128].reshape(heads * HALF, 128).astype(jnp.bfloat16)
                )
                ms, ls = stats[slot, half, 0], stats[slot, half, 1]
                for hh in range(heads):
                    here = lane == k * 8 + part * heads + hh
                    ms = jnp.where(here, m3[hh, cut], ms)
                    ls = jnp.where(here, o3[hh, cut, 128:], ls)
                stats[slot, half, 0] = ms
                stats[slot, half, 1] = ls

    def quarter(t, carry):
        @pl.when(t == 1)
        def _():
            for o in range(GROUPS):
                spread(o, xpart, xs, xr, q).wait_recv()
                spread(o, xpart, fs, fr, core).start()
            for o in range(GROUPS):
                spread(o, core, cs, cr, q).wait_recv()

        @pl.when(t == 3)
        def _():
            for o in range(GROUPS):
                spread(o, xcore, fs, fr, q).wait_recv()

        holder = ((xx + t // 2) % 2) * 2 + (cc + t) % 2
        own = jnp.where(t == 0, 1, 0).astype(jnp.int32)

        def one(n, inner):
            k = holder * 2 + n % 2
            slot = (xx + 1 + n // 2) % 2
            step(slot, k, own)

            @pl.when(n < 2)
            def _():
                acc_send(slot, 0, k, os0, (1 - xx) * 2).start()
                acc_send(slot, 1, k, os1, (1 - xx) * 2 + 1).start()

            @pl.when(n >= 2)
            def _():
                acc_send(slot, 1 - cc, k, os2, core).start()

            return inner

        return lax.fori_loop(0, 4, one, carry)

    lax.fori_loop(0, 4, quarter, 0)

    def stat_send(slot, half, n, to):
        return remote(stats.at[slot, half], rstat.at[q], ss.at[n], srs.at[q], (g, to))

    stat_send(1 - xx, 0, 0, (1 - xx) * 2).start()
    stat_send(1 - xx, 1, 1, (1 - xx) * 2 + 1).start()
    stat_send(xx, 1 - cc, 2, core).start()

    def from_stat(other):
        return remote(stats.at[0, 0], rstat.at[other], ss.at[0], srs.at[other], (g, q))

    for other in (core, xpart, xcore):
        from_stat(other).wait_recv()
    tops = [stats[xx, cc, 0]] + [rstat[other, 0] for other in (core, xpart, xcore)]
    sums = [stats[xx, cc, 1]] + [rstat[other, 1] for other in (core, xpart, xcore)]
    top = functools.reduce(jnp.maximum, tops)
    factors = [jnp.exp2((m - top) * SCALE2) for m in tops]
    total = sum(f * l for f, l in zip(factors, sums))
    factors = [f / total for f in factors]

    for k in range(8):
        for other in (core, xpart, xcore):
            remote(accs.at[0, 0, k], rbuf.at[other, k], os0.at[k], ors.at[other, k], (g, q)).wait_recv()
        terms = [accs[xx, cc, k]] + [rbuf[other, k] for other in (core, xpart, xcore)]
        terms = [term.astype(jnp.float32).reshape(8, HALF, 128) for term in terms]
        for hh in range(8):
            h = k * 8 + hh
            value = sum(f[:, h : h + 1] * term[hh] for f, term in zip(factors, terms))
            out_ref[:, h * 128 : (h + 1) * 128] = value.astype(jnp.bfloat16)

    for o in range(1, GROUPS):
        first_q(o).wait_send()
        second_q(o).wait_send()

        @pl.when(relays(lax.rem(g + o, GROUPS)))
        def _():
            first_d(o).wait_send()

        @pl.when(relays(g))
        def _():
            second_d(o).wait_send()

    for o in range(GROUPS):
        spread(o, q, xs, xr, xpart).wait_send()
        spread(o, q, cs, cr, core).wait_send()
        spread(o, xpart, fs, fr, core).wait_send()
    for k in range(8):
        acc_send(1 - xx, 0, k, os0, (1 - xx) * 2).wait_send()
        acc_send(1 - xx, 1, k, os1, (1 - xx) * 2 + 1).wait_send()
        acc_send(xx, 1 - cc, k, os2, core).wait_send()
    stat_send(1 - xx, 0, 0, (1 - xx) * 2).wait_send()
    stat_send(1 - xx, 1, 1, (1 - xx) * 2 + 1).wait_send()
    stat_send(xx, 1 - cc, 2, core).wait_send()


def fused(queries, draft_key_value, kv_cache, cache_lengths, ancestors, dealing):
    dma = pltpu.SemaphoreType.DMA
    bf = jnp.bfloat16
    vm = pl.BlockSpec(memory_space=pltpu.VMEM)
    sm = pl.BlockSpec(memory_space=pltpu.SMEM)
    return pl.pallas_call(
        fused_kernel,
        out_shape=jax.ShapeDtypeStruct((HALF, 8192), bf),
        in_specs=[sm, sm, vm, vm, pl.BlockSpec(memory_space=pl.ANY), vm],
        out_specs=vm,
        scratch_shapes=[
            pltpu.VMEM((16, TOK, 256), bf),
            pltpu.VMEM((16, TOK, 128), bf),
            pltpu.VMEM((GROUPS, 2, 2, TOK, 128), bf),
            pltpu.VMEM((GROUPS, 2, TOK, 128), bf),
            pltpu.VMEM((2, 64, TOK, 128), bf),
            pltpu.VMEM((2, 4, TOK, 128), bf),
            pltpu.VMEM((16, 2048, 256), bf),
            pltpu.VMEM((2, 2, 8, ROWS, 128), bf),
            pltpu.VMEM((QUARTERS, 8, ROWS, 128), bf),
            pltpu.VMEM((2, 2, 2, HALF, 128), jnp.float32),
            pltpu.VMEM((QUARTERS, 2, HALF, 128), jnp.float32),
        ]
        + [dma((GROUPS,))] * 14
        + [dma((16,)), dma((8,)), dma((8,)), dma((8,)), dma((QUARTERS, 8)), dma((3,)), dma((QUARTERS,))],
        compiler_params=pltpu.CompilerParams(
            collective_id=0, has_side_effects=True, vmem_limit_bytes=56 * 1024 * 1024
        ),
        cost_estimate=pl.CostEstimate(flops=2 * 10**9, bytes_accessed=18 * 10**6, transcendentals=13 * 10**6),
    )(dealing, cache_lengths, queries, draft_key_value, kv_cache, ancestors)


def body(groups, quarters, queries, draft_key_value, kv_cache, cache_lengths, ancestors, dealing, accepted_path):
    args = (queries, draft_key_value, kv_cache, cache_lengths, ancestors, dealing, accepted_path)
    fits = (
        groups == GROUPS
        and quarters == QUARTERS
        and queries.shape == (2, TOK, 2048)
        and kv_cache.shape == (2, 2048, 2048)
    )
    if not fits:
        return plain_body(*args)
    picker = (
        accepted_path[:, :, None] == jnp.arange(TOK, dtype=jnp.int32)[None, None, :]
    ).astype(jnp.bfloat16)
    kept_entries = jnp.einsum(
        "rit,rtc->ric", picker, draft_key_value, preferred_element_type=jnp.float32
    ).astype(jnp.bfloat16)
    context = fused(queries, draft_key_value, kv_cache, cache_lengths, ancestors, dealing)
    return (context, kept_entries)


def solution(mesh):
    placed = (
        P("req", None, "seq"),
        P("req", None, "seq"),
        P("req", "seq", None),
        P("req"),
        P("req", None, None),
        P(),
        P("req", None),
    )
    return jax.shard_map(
        functools.partial(body, mesh.shape["req"], mesh.shape["seq"]),
        mesh=mesh,
        in_specs=placed,
        out_specs=(P(("req", "seq"), None), P("req", None, "seq")),
        check_vma=False,
    )
```

```python
import functools
import math

import jax
import jax.numpy as jnp
from jax import lax
from jax.experimental import pallas as pl
from jax.experimental.pallas import tpu as pltpu
from jax.sharding import PartitionSpec as P

HEAD_WIDTH = 128
BLK = 1024


def online_merge(earlier, later):
    max_a, sum_a, acc_a = earlier
    max_b, sum_b, acc_b = later
    row_max = jnp.maximum(max_a, max_b)
    scale_a = jnp.exp(max_a - row_max)
    scale_b = jnp.exp(max_b - row_max)
    return (
        row_max,
        sum_a * scale_a + sum_b * scale_b,
        acc_a * scale_a[..., None] + acc_b * scale_b[..., None],
    )


def block_terms(grouped, key_rows, values, allowed):
    scores = jnp.einsum(
        "tkgd,skd->tkgs", grouped, key_rows, preferred_element_type=jnp.float32
    ) * HEAD_WIDTH ** (-0.5)
    scores = jnp.where(allowed, scores, jnp.float32(-1e30))
    row_max = jnp.max(scores, axis=-1)
    weights = jnp.where(allowed, jnp.exp(scores - row_max[..., None]), jnp.float32(0.0))
    row_sum = jnp.sum(weights, axis=-1)
    row_acc = jnp.einsum(
        "tkgs,skd->tkgd", weights.astype(jnp.bfloat16), values, preferred_element_type=jnp.float32
    )
    return (row_max, row_sum, row_acc)


def attend(query_rows, cache_rows, draft_rows, length, pos_offset, tree_mask, use_draft, blk_size):
    tree_len = query_rows.shape[0]
    kv_heads = cache_rows.shape[1] // (2 * HEAD_WIDTH)
    groups = query_rows.shape[1] // (HEAD_WIDTH * kv_heads)
    grouped = query_rows.reshape(tree_len, kv_heads, groups, HEAD_WIDTH)
    draft_part = draft_rows.reshape(tree_len, kv_heads, 2, HEAD_WIDTH)
    draft_allowed = jnp.logical_and(tree_mask > 0, use_draft)[:, None, None, :]
    running = block_terms(grouped, draft_part[:, :, 0], draft_part[:, :, 1], draft_allowed)
    blk_count = cache_rows.shape[0] // blk_size

    def body_step(blk_index, state):
        blk_start = blk_index * blk_size

        def absorb(state_in):
            cache_piece = lax.dynamic_slice_in_dim(cache_rows, blk_start, blk_size, 0).reshape(
                blk_size, kv_heads, 2, HEAD_WIDTH
            )
            positions = pos_offset + blk_start + jnp.arange(blk_size, dtype=jnp.int32)
            allowed = (positions < length)[None, None, None, :]
            return online_merge(
                state_in, block_terms(grouped, cache_piece[:, :, 0], cache_piece[:, :, 1], allowed)
            )

        return lax.cond(pos_offset + blk_start < length, absorb, lambda state_in: state_in, state)

    return lax.fori_loop(0, blk_count, body_step, running)


def plain_body(queries, draft_key_value, kv_cache, cache_lengths, ancestors, dealing, accepted_path):
    local_reqs = kv_cache.shape[0]
    tree_len = queries.shape[1]
    picker = (
        accepted_path[:, :, None] == jnp.arange(tree_len, dtype=jnp.int32)[None, None, :]
    ).astype(jnp.bfloat16)
    kept_entries = jnp.einsum(
        "rit,rtc->ric", picker, draft_key_value, preferred_element_type=jnp.float32
    ).astype(jnp.bfloat16)
    every_query, every_draft = (
        lax.all_gather(queries, "req", axis=0, tiled=True),
        lax.all_gather(draft_key_value, "req", axis=0, tiled=True),
    )
    chosen = lax.dynamic_slice_in_dim(dealing, lax.axis_index("req") * local_reqs, local_reqs)
    own_query = jnp.stack(
        [
            lax.dynamic_index_in_dim(every_query, chosen[slot], 0, keepdims=False)
            for slot in range(local_reqs)
        ],
        axis=0,
    )
    own_draft = jnp.stack(
        [
            lax.dynamic_index_in_dim(every_draft, chosen[slot], 0, keepdims=False)
            for slot in range(local_reqs)
        ],
        axis=0,
    )
    seq_count = lax.axis_size("seq")
    full_query, full_draft = (
        lax.all_gather(own_query, "seq", axis=2, tiled=True),
        lax.all_gather(own_draft, "seq", axis=2, tiled=True),
    )
    position = lax.axis_index("seq")
    pos_offset = position * kv_cache.shape[1]
    maxima, sums, partials = ([], [], [])
    for slot_index in range(local_reqs):
        row_max, row_sum, row_acc = attend(
            full_query[slot_index],
            kv_cache[slot_index],
            full_draft[slot_index],
            cache_lengths[slot_index],
            pos_offset,
            ancestors[slot_index],
            position == 0,
            BLK,
        )
        maxima.append(row_max.reshape(tree_len, -1))
        sums.append(row_sum.reshape(tree_len, -1))
        partials.append(row_acc.reshape(tree_len, -1))
    all_max = jnp.concatenate(maxima, axis=0)
    all_sum = jnp.concatenate(sums, axis=0)
    all_acc = jnp.concatenate(partials, axis=0)
    head_count = all_max.shape[1]
    recv_acc, recv_max, recv_sum = (
        lax.all_to_all(all_acc[None], "seq", split_axis=1, concat_axis=0, tiled=True),
        lax.all_to_all(all_max[None], "seq", split_axis=1, concat_axis=0, tiled=True),
        lax.all_to_all(all_sum[None], "seq", split_axis=1, concat_axis=0, tiled=True),
    )
    top_max = jnp.max(recv_max, axis=0)
    factors = jnp.exp(recv_max - top_max[None])
    denominator = jnp.sum(factors * recv_sum, axis=0)
    token_count = recv_acc.shape[1]
    numerator = jnp.sum(
        factors[..., None] * recv_acc.reshape(seq_count, token_count, head_count, HEAD_WIDTH),
        axis=0,
    )
    context = (
        (numerator / denominator[..., None])
        .reshape(token_count, head_count * HEAD_WIDTH)
        .astype(jnp.bfloat16)
    )
    return (context, kept_entries)


MESH = pl.DeviceIdType.MESH
TOK = 48
HALF = TOK // 2
ROWS = 8 * HALF
NEG = -1e30
SCALE2 = HEAD_WIDTH ** (-0.5) * math.log2(math.e)
GROUPS = 8
QUARTERS = 4
ROW_CHUNKS = 2


def fused_kernel(
    deal, lens, q_ref, d_ref, kv_ref, anc_ref, out_ref,
    r1q, r1d, s2q, s2d, qf, df, kvb, accs, rbuf, stats, rstat,
    s1, r1, s1d, r1ds, s2, r2, s2ds, r2ds, xs, xr, kvs, ks, kr,
    os0, os1, os2, ors, ss, srs,
):
    g = lax.axis_index("req")
    q = lax.axis_index("seq")
    xx, cc = q // 2, q % 2
    core = xx * 2 + (1 - cc)
    xpart = (1 - xx) * 2 + cc
    xcore = (1 - xx) * 2 + (1 - cc)

    barrier = pltpu.get_barrier_semaphore()
    for o in range(1, GROUPS):
        pl.semaphore_signal(barrier, inc=1, device_id=(lax.rem(g + o, GROUPS), q), device_id_type=MESH)
    for other in (core, xpart, xcore):
        pl.semaphore_signal(barrier, inc=1, device_id=(g, other), device_id_type=MESH)
    pl.semaphore_wait(barrier, GROUPS + 2)

    def relays(i):
        return i % 2 == (i // 2) % 2

    def remote(src, dst, send, recv, dev):
        return pltpu.make_async_remote_copy(
            src_ref=src, dst_ref=dst, send_sem=send, recv_sem=recv, device_id=dev, device_id_type=MESH
        )

    def first_q(o):
        i = lax.rem(g + o, GROUPS)
        return remote(
            q_ref.at[:, :, pl.ds(pl.multiple_of(i * 256, 256), 256)], r1q.at[pl.ds(2 * g, 2)],
            s1.at[o], r1.at[o], (i, q),
        )

    def first_d(o):
        i = lax.rem(g + o, GROUPS)
        return remote(
            d_ref.at[:, :, pl.ds(pl.multiple_of((i // 2) * 128, 128), 128)], r1d.at[pl.ds(2 * g, 2)],
            s1d.at[o], r1ds.at[o], (i, q),
        )

    def columns(parity, kl):
        k = 2 * parity + 4 * (kl // 2) + kl % 2
        return pl.ds(pl.multiple_of(k * 256, 256), 256)

    def kv_copy(slot, kl):
        return pltpu.make_async_copy(
            kv_ref.at[slot, :, columns(cc, kl)], kvb.at[slot * 4 + kl, cc], kvs.at[slot * 4 + kl]
        )

    def kv_swap(slot, kl):
        n = slot * 4 + kl
        return remote(
            kv_ref.at[slot, :, columns(1 - cc, kl)], kvb.at[n, cc], ks.at[n], kr.at[n], (g, core)
        )

    def kv_arrival(slot, kl):
        n = slot * 4 + kl
        return remote(
            kv_ref.at[slot, :, columns(cc, kl)], kvb.at[n, 1 - cc], ks.at[n], kr.at[n], (g, core)
        )

    for o in range(1, GROUPS):
        first_q(o).start()

        @pl.when(relays(lax.rem(g + o, GROUPS)))
        def _():
            first_d(o).start()

    def start_kv(n, carry):
        kv_swap(n // 4, n % 4).start()
        kv_copy(n // 4, n % 4).start()
        return carry

    lax.fori_loop(0, 8, start_kv, 0)
    r1q[pl.ds(2 * g, 2)] = q_ref[:, :, pl.ds(pl.multiple_of(g * 256, 256), 256)]
    r1d[pl.ds(2 * g, 2)] = d_ref[:, :, pl.ds(pl.multiple_of((g // 2) * 128, 128), 128)]
    for part in range(2):
        for half in range(2):
            stats[part, half] = jnp.ones_like(stats[part, half])

    for o in range(1, GROUPS):
        first_q(o).wait_recv()

        @pl.when(relays(g))
        def _():
            first_d(o).wait_recv()

    def second_q(o):
        d = lax.rem(g + o, GROUPS)
        return remote(
            s2q.at[d], qf.at[:, pl.ds(q * 16 + g * 2, 2)], s2.at[o], r2.at[o], (d, q)
        )

    def second_d(o):
        d = lax.rem(g + o, GROUPS)
        return remote(s2d.at[d], df.at[:, g // 2], s2ds.at[o], r2ds.at[o], (d, q))

    for o in list(range(1, GROUPS)) + [0]:
        d = lax.rem(g + o, GROUPS)
        for j in range(2):
            r = deal[2 * d + j]
            piece = r1q[r]
            if o == 0:
                qf[j, q * 16 + g * 2] = piece[:, :128]
                qf[j, q * 16 + g * 2 + 1] = piece[:, 128:]
            else:
                s2q[d, j, 0] = piece[:, :128]
                s2q[d, j, 1] = piece[:, 128:]
        if o:
            second_q(o).start()

        @pl.when(relays(g))
        def _():
            for j in range(2):
                r = deal[2 * d + j]
                if o == 0:
                    df[j, g // 2] = r1d[r]
                else:
                    s2d[d, j] = r1d[r]
            if o:
                second_d(o).start()

    def spread(o, owner, send, recv, to):
        src = lax.rem(g + GROUPS - o, GROUPS)
        part = qf.at[:, pl.ds(owner * 16 + src * 2, 2)]
        return remote(part, part, send.at[o], recv.at[o], (g, to))

    for o in range(GROUPS):
        if o:
            second_q(o).wait_recv()
        spread(o, q, xs, xr, xpart).start()
    for o in range(1, GROUPS):

        @pl.when(relays(lax.rem(g + GROUPS - o, GROUPS)))
        def _():
            second_d(o).wait_recv()

    def acc_send(slot, half, kl, sem, to):
        return remote(accs.at[slot, half, kl], rbuf.at[q, kl], sem.at[kl], ors.at[q, kl], (g, to))

    def step(slot, k, kl, own):
        kv_copy(slot, kl).wait()
        kv_arrival(slot, kl).wait_recv()
        ones = jnp.ones((2048, 128), jnp.bfloat16)
        where_pos = lax.broadcasted_iota(jnp.int32, (1, 2048), 1) + xx * 4096
        tree = jnp.where(
            jnp.logical_and(anc_ref[slot] > 0, jnp.full((TOK, TOK), own, jnp.int32) > 0),
            jnp.float32(0.0), jnp.float32(NEG),
        )
        dk = df[slot, (k % 2) * 2]
        dv = jnp.concatenate([df[slot, (k % 2) * 2 + 1], jnp.ones((TOK, 128), jnp.bfloat16)], axis=1)
        lane = lax.broadcasted_iota(jnp.int32, (HALF, 128), 1)
        heads = 8 // ROW_CHUNKS
        rows = heads * TOK
        contract = (((1,), (1,)), ((), ()))
        plain = (((1,), (0,)), ((), ()))
        for part in range(ROW_CHUNKS):
            qs = qf[slot, pl.ds(k * 8 + part * heads, heads)].reshape(rows, 128)
            t = lax.dot_general(qs, dk, contract, preferred_element_type=jnp.float32)
            t = (t.reshape(heads, TOK, TOK) + tree[None]).reshape(rows, TOK)
            m = jnp.max(t, axis=1, keepdims=True)
            scores = []
            for b in range(2):
                s = lax.dot_general(
                    qs, kvb[slot * 4 + kl, b, :, :128], contract, preferred_element_type=jnp.float32
                ) + jnp.where(where_pos + b * 2048 < lens[slot], jnp.float32(0.0), jnp.float32(NEG))
                m = jnp.maximum(m, jnp.max(s, axis=1, keepdims=True))
                scores.append(s)
            pt = jnp.exp2((t - m) * SCALE2).astype(jnp.bfloat16)
            o = lax.dot_general(pt, dv, plain, preferred_element_type=jnp.float32)
            for b in range(2):
                p = jnp.exp2((scores[b] - m) * SCALE2).astype(jnp.bfloat16)
                values = jnp.concatenate([kvb[slot * 4 + kl, b, :, 128:], ones], axis=1)
                o = o + lax.dot_general(p, values, plain, preferred_element_type=jnp.float32)
            o3 = o.reshape(heads, TOK, 256)
            m3 = jnp.broadcast_to(m, (rows, 128)).reshape(heads, TOK, 128)
            for half in range(2):
                cut = slice(half * HALF, (half + 1) * HALF)
                accs[slot, half, kl, pl.ds(part * heads * HALF, heads * HALF)] = (
                    o3[:, cut, :128].reshape(heads * HALF, 128).astype(jnp.bfloat16)
                )
                ms, ls = stats[slot, half, 0], stats[slot, half, 1]
                for hh in range(heads):
                    here = lane == k * 8 + part * heads + hh
                    ms = jnp.where(here, m3[hh, cut], ms)
                    ls = jnp.where(here, o3[hh, cut, 128:], ls)
                stats[slot, half, 0] = ms
                stats[slot, half, 1] = ls

    def stage(t, carry):
        @pl.when(t == 1)
        def _():
            for o in range(GROUPS):
                spread(o, xpart, xs, xr, q).wait_recv()

        column = (xx + t) % 2
        own = 1 - t

        def one(n, inner):
            k = (column * 2 + cc) * 2 + n % 2
            kl = column * 2 + n % 2
            slot = (xx + 1 + n // 2) % 2
            step(slot, k, kl, own)

            @pl.when(n < 2)
            def _():
                acc_send(slot, 0, kl, os0, (1 - xx) * 2).start()
                acc_send(slot, 1, kl, os1, (1 - xx) * 2 + 1).start()

            @pl.when(n >= 2)
            def _():
                acc_send(slot, 1 - cc, kl, os2, core).start()

            return inner

        return lax.fori_loop(0, 4, one, carry)

    lax.fori_loop(0, 2, stage, 0)

    def stat_send(slot, half, n, to):
        return remote(stats.at[slot, half], rstat.at[q], ss.at[n], srs.at[q], (g, to))

    stat_send(1 - xx, 0, 0, (1 - xx) * 2).start()
    stat_send(1 - xx, 1, 1, (1 - xx) * 2 + 1).start()
    stat_send(xx, 1 - cc, 2, core).start()

    def from_stat(other):
        return remote(stats.at[0, 0], rstat.at[other], ss.at[0], srs.at[other], (g, q))

    for other in (core, xpart, xcore):
        from_stat(other).wait_recv()
    rstat[q] = stats[xx, cc]
    rbuf[q] = accs[xx, cc]
    factors = []
    for parity in range(2):
        pair = (xx * 2 + parity, (1 - xx) * 2 + parity)
        tops = [rstat[other, 0] for other in pair]
        top = jnp.maximum(tops[0], tops[1])
        scaled = [jnp.exp2((m - top) * SCALE2) for m in tops]
        total = scaled[0] * rstat[pair[0], 1] + scaled[1] * rstat[pair[1], 1]
        factors.append([f / total for f in scaled])

    for kl in range(4):
        for other in (core, xpart, xcore):
            remote(accs.at[0, 0, kl], rbuf.at[other, kl], os0.at[kl], ors.at[other, kl], (g, q)).wait_recv()
    for k in range(8):
        parity, kl = (k // 2) % 2, (k // 4) * 2 + k % 2
        terms = [rbuf[xx * 2 + parity, kl], rbuf[(1 - xx) * 2 + parity, kl]]
        terms = [term.astype(jnp.float32).reshape(8, HALF, 128) for term in terms]
        for hh in range(8):
            h = k * 8 + hh
            value = sum(f[:, h : h + 1] * term[hh] for f, term in zip(factors[parity], terms))
            out_ref[:, h * 128 : (h + 1) * 128] = value.astype(jnp.bfloat16)

    for o in range(1, GROUPS):
        first_q(o).wait_send()
        second_q(o).wait_send()

        @pl.when(relays(lax.rem(g + o, GROUPS)))
        def _():
            first_d(o).wait_send()

        @pl.when(relays(g))
        def _():
            second_d(o).wait_send()

    for o in range(GROUPS):
        spread(o, q, xs, xr, xpart).wait_send()
    for n in range(8):
        kv_swap(n // 4, n % 4).wait_send()
    for k in range(4):
        acc_send(1 - xx, 0, k, os0, (1 - xx) * 2).wait_send()
        acc_send(1 - xx, 1, k, os1, (1 - xx) * 2 + 1).wait_send()
        acc_send(xx, 1 - cc, k, os2, core).wait_send()
    stat_send(1 - xx, 0, 0, (1 - xx) * 2).wait_send()
    stat_send(1 - xx, 1, 1, (1 - xx) * 2 + 1).wait_send()
    stat_send(xx, 1 - cc, 2, core).wait_send()


def fused(queries, draft_key_value, kv_cache, cache_lengths, ancestors, dealing):
    dma = pltpu.SemaphoreType.DMA
    bf = jnp.bfloat16
    vm = pl.BlockSpec(memory_space=pltpu.VMEM)
    sm = pl.BlockSpec(memory_space=pltpu.SMEM)
    return pl.pallas_call(
        fused_kernel,
        out_shape=jax.ShapeDtypeStruct((HALF, 8192), bf),
        in_specs=[sm, sm, vm, vm, pl.BlockSpec(memory_space=pl.ANY), vm],
        out_specs=vm,
        scratch_shapes=[
            pltpu.VMEM((16, TOK, 256), bf),
            pltpu.VMEM((16, TOK, 128), bf),
            pltpu.VMEM((GROUPS, 2, 2, TOK, 128), bf),
            pltpu.VMEM((GROUPS, 2, TOK, 128), bf),
            pltpu.VMEM((2, 64, TOK, 128), bf),
            pltpu.VMEM((2, 4, TOK, 128), bf),
            pltpu.VMEM((8, 2, 2048, 256), bf),
            pltpu.VMEM((2, 2, 4, ROWS, 128), bf),
            pltpu.VMEM((QUARTERS, 4, ROWS, 128), bf),
            pltpu.VMEM((2, 2, 2, HALF, 128), jnp.float32),
            pltpu.VMEM((QUARTERS, 2, HALF, 128), jnp.float32),
        ]
        + [dma((GROUPS,))] * 10
        + [dma((8,))] * 3
        + [dma((4,)), dma((4,)), dma((4,)), dma((QUARTERS, 4)), dma((3,)), dma((QUARTERS,))],
        compiler_params=pltpu.CompilerParams(
            collective_id=0, has_side_effects=True, vmem_limit_bytes=56 * 1024 * 1024
        ),
        cost_estimate=pl.CostEstimate(flops=2 * 10**9, bytes_accessed=18 * 10**6, transcendentals=13 * 10**6),
    )(dealing, cache_lengths, queries, draft_key_value, kv_cache, ancestors)


def body(groups, quarters, queries, draft_key_value, kv_cache, cache_lengths, ancestors, dealing, accepted_path):
    args = (queries, draft_key_value, kv_cache, cache_lengths, ancestors, dealing, accepted_path)
    fits = (
        groups == GROUPS
        and quarters == QUARTERS
        and queries.shape == (2, TOK, 2048)
        and kv_cache.shape == (2, 2048, 2048)
    )
    if not fits:
        return plain_body(*args)
    picker = (
        accepted_path[:, :, None] == jnp.arange(TOK, dtype=jnp.int32)[None, None, :]
    ).astype(jnp.bfloat16)
    kept_entries = jnp.einsum(
        "rit,rtc->ric", picker, draft_key_value, preferred_element_type=jnp.float32
    ).astype(jnp.bfloat16)
    context = fused(queries, draft_key_value, kv_cache, cache_lengths, ancestors, dealing)
    return (context, kept_entries)


def solution(mesh):
    placed = (
        P("req", None, "seq"),
        P("req", None, "seq"),
        P("req", "seq", None),
        P("req"),
        P("req", None, None),
        P(),
        P("req", None),
    )
    return jax.shard_map(
        functools.partial(body, mesh.shape["req"], mesh.shape["seq"]),
        mesh=mesh,
        in_specs=placed,
        out_specs=(P(("req", "seq"), None), P("req", None, "seq")),
        check_vma=False,
    )
```
